32 devices in a mesh: row: 4 (over y, x), col: 8 (over z, core).
Axes of the slice: x: 2, y: 2, z: 4, core: 2. Of those that a mesh axis runs over, the one named last changes fastest.
Arguments:
- beats: bfloat16 [65536, 128], P(('row', 'col')), may hold values from -6 to 6
- track_marks: int32 [65536], P(('row', 'col')), may hold values 0 or 1
- valid_beats: int32 [32], replicated, may hold values from 64 to 2048, as said below
- pairing: int32 [2, 32], replicated, may hold values from 0 to 31, as said below
Outputs:
- profile: float32 [65536], P(('row', 'col'))
The draws below stay inside these ranges and needn't reach their ends.
Inputs may be any that keep to these rules, and one draw needn't show every extreme that they name: `valid_beats`: each segment has at least 64 valid beats; some segment is full in every draw. pairing[0] pairs the segments of each grid column among themselves and pairing[1] those of each grid row; each row of pairing is an involution without fixed points.
All inputs are finite; a program needn't handle non-finite values. No bound on the sum of `track_marks` on one device may be relied on, other than what follows from the above.
Results may differ from the reference program's by a relative error of at most 0.0003.
Values may be sent and summed in bfloat16 or wider, within the bound.
A program may use at most 128 MiB of HBM per device.

```python
import jax
import jax.numpy as jnp
from jax import lax

WIDTH = 128
SPAN = 64
SEG_BEATS = 2048
ROW_SEGS = 4
COL_SEGS = 8
SEGS = 32
BEATS = 65536


def draw_valid_beats(key, part):
    counts = jax.random.randint(jax.random.fold_in(key, 11), (SEGS,), SPAN, SEG_BEATS)
    whole = jax.random.randint(jax.random.fold_in(key, 12), (SEGS,), 0, 2)
    counts = jnp.where(whole == 1, SEG_BEATS, counts)
    return counts.at[0].set(SEG_BEATS).astype(jnp.int32)


def pair_within(key, groups, members):
    keys = jax.random.split(key, groups)
    orders = jax.vmap(lambda single: jax.random.permutation(single, members))(keys)
    mates = orders[:, jnp.arange(members) ^ 1]
    result = jnp.zeros((groups, members), jnp.int32)
    group_ids = jnp.arange(groups)[:, None] * jnp.ones((1, members), jnp.int32)
    return result.at[group_ids, orders].set(mates.astype(jnp.int32))


def draw_pairing(key, part):
    column_mates = pair_within(jax.random.fold_in(key, 21), COL_SEGS, ROW_SEGS)
    row_mates = pair_within(jax.random.fold_in(key, 22), ROW_SEGS, COL_SEGS)
    grid_rows = jnp.arange(ROW_SEGS, dtype=jnp.int32)[:, None]
    grid_cols = jnp.arange(COL_SEGS, dtype=jnp.int32)[None, :]
    first = column_mates.T * COL_SEGS + grid_cols
    second = grid_rows * COL_SEGS + row_mates
    return jnp.stack([first.reshape(SEGS), second.reshape(SEGS)], 0).astype(jnp.int32)


def touch_ends(drawn, own_key, smallest, largest):
    spot = [jax.random.randint(jax.random.fold_in(own_key, axis), (), 0, length) for axis, length in enumerate(drawn.shape)]
    widest = drawn.shape.index(max(drawn.shape))
    next_to = spot[:widest] + [(spot[widest] + 1) % drawn.shape[widest]] + spot[widest + 1:]
    return drawn.at[tuple(spot)].set(smallest).at[tuple(next_to)].set(largest)


def block_levels(stream_key, extent, cuts, least, top_value):
    def one(dim, parts):
        steps = jax.random.uniform(jax.random.fold_in(jax.random.fold_in(stream_key, 6), dim), (parts,), jnp.float32, least / len(cuts), top_value / len(cuts))
        return jnp.repeat(jnp.exp(steps), extent[dim] // parts).reshape((-1,) + (1,) * (len(extent) - dim - 1))

    level = one(*cuts[0])
    for cut in cuts[1:]:
        level = level * one(*cut)
    return level


def centred(stream_key, shape, deviation, reach, cuts=(), kind=jnp.bfloat16):
    loudness = block_levels(stream_key, shape, cuts, -0.22, 0.18) if cuts else 1.0
    drawn = jax.random.normal(stream_key, shape, jnp.float32) * deviation * loudness
    return jnp.minimum(jnp.maximum(drawn, -reach), reach).astype(kind)


def setup_inputs(seed: int = 0) -> dict:
    key_of = jax.random.split(jax.random.key(seed), 5)
    beats = centred(key_of[0], (BEATS, WIDTH), 1.0, 6.0, ((0, 32),))
    track_marks = touch_ends((jax.random.randint(key_of[1], (BEATS,), 0, 256) < 1).astype(jnp.int32), jax.random.fold_in(key_of[1], 1), 0, 1)
    valid_beats = draw_valid_beats(jax.random.fold_in(key_of[4], 71), 0)
    pairing = draw_pairing(jax.random.fold_in(key_of[4], 71), 0)
    return dict(beats=beats, track_marks=track_marks, valid_beats=valid_beats, pairing=pairing)


CEIL = 4.0


def window_sum(values):
    total = values[..., 0:SEG_BEATS]
    for shift in range(1, SPAN):
        total = total + values[..., shift:shift + SEG_BEATS]
    return total


def reference(beats, track_marks, valid_beats, pairing):
    seg_beats = beats.reshape(SEGS, SEG_BEATS, WIDTH)
    following = jnp.concatenate([seg_beats[1:, :SPAN], jnp.zeros((1, SPAN, WIDTH), beats.dtype)], 0)
    extended = jnp.concatenate([seg_beats, following], 1).astype(jnp.float32)
    marks = track_marks.astype(jnp.float32).reshape(SEGS, SEG_BEATS)
    mark_next = jnp.concatenate([marks[1:, :SPAN], jnp.zeros((1, SPAN), jnp.float32)], 0)
    mark_ext = jnp.concatenate([marks, mark_next], 1)
    crossed = mark_ext[:, 1:1 + SEG_BEATS]
    for shift in range(2, SPAN):
        crossed = crossed + mark_ext[:, shift:shift + SEG_BEATS]
    offsets = jnp.arange(SEG_BEATS, dtype=jnp.int32)
    segment_ids = jnp.arange(SEGS, dtype=jnp.int32)
    within = offsets[None, :] + (SPAN - 1) < valid_beats[:, None]
    crossing = (valid_beats == SEG_BEATS) & (segment_ids < SEGS - 1)
    live = (within | crossing[:, None]) & (crossed < 0.5)
    norms = window_sum(jnp.sum(extended * extended, axis=2))

    def row_minima(owner, other):
        left = extended[owner, :SEG_BEATS + SPAN - 1]
        right = extended[other, :SEG_BEATS + SPAN - 1]
        gram = jnp.dot(left, right.T, precision=lax.Precision.HIGHEST)

        def accumulate(shift, total):
            return total + lax.dynamic_slice(gram, (shift, shift), (SEG_BEATS, SEG_BEATS))

        dots = lax.fori_loop(0, SPAN, accumulate, jnp.zeros((SEG_BEATS, SEG_BEATS), jnp.float32))
        dist = (norms[owner][:, None] + norms[other][None, :] - 2.0 * dots) / (SPAN * WIDTH)
        pos_own = (owner * SEG_BEATS + offsets).astype(jnp.int32)
        pos_other = (other * SEG_BEATS + offsets).astype(jnp.int32)
        allowed = live[owner][:, None] & live[other][None, :] & (jnp.abs(pos_own[:, None] - pos_other[None, :]) >= SPAN // 2)
        return jnp.min(jnp.where(allowed, dist, CEIL), axis=1)

    def one_segment(owner):
        first = row_minima(owner, pairing[0, owner])
        second = row_minima(owner, pairing[1, owner])
        return jnp.minimum(first, second)

    profile = lax.map(one_segment, segment_ids)
    return profile.reshape(BEATS)
```

```python
import functools

import jax
import jax.numpy as jnp
from jax import lax
from jax.experimental import pallas as pl
from jax.experimental.pallas import tpu as pltpu
from jax.sharding import PartitionSpec as P

SPAN = 64
CEIL = 4.0
BIG = 1e9
LANES = 128
SUB = 8
HIGH = LANES // SUB
LEAD = 4


def from_behind(block, axis, distance):
    devices = range(lax.axis_size(axis))
    route = [(i - distance, i) for i in devices if i - distance in devices]
    return lax.ppermute(block, axis, route)


def window_sum(values, count):
    layered = values
    window = 1
    while window < SPAN:
        layered = layered[:-window] + layered[window:]
        window = window * 2
    return layered[:count]


def meet_kernel(
    rows, tiles, x_ref, y_ref, na_ref, nb_ref, pen_ref, ro_ref, co_ref,
    xf, yf, x8, y8, ga, gb, gc, a10, a11, a20, a21, a22, a23, nab, rm,
):
    width = x_ref.shape[1]
    x_rows = x8.shape[0]
    steps = (tiles + 8) // 4
    a1c = (a10, a11)
    a2c = (a20, a21, a22, a23)
    gram = (ga, gb)
    shift0 = 4 * steps
    chains = rows + 12
    half = chains // 2

    xf[...] = jnp.zeros_like(xf)
    xf[: x_ref.shape[0], :] = x_ref[...].astype(jnp.float32) * -2.0
    yf[:SUB, :] = jnp.zeros((SUB, width), jnp.float32)
    yf[SUB : SUB + y_ref.shape[0], :] = y_ref[...].astype(jnp.float32)
    for ref in (gc,) + a1c + a2c:
        ref[...] = jnp.zeros_like(ref)
    for ref in gram:
        ref[: LEAD * SUB, :] = jnp.zeros((LEAD * SUB, ref.shape[1]), jnp.float32)
    nab[...] = jnp.full_like(nab, BIG)
    nab[16 * SUB : (16 + rows) * SUB, :] = jnp.broadcast_to(na_ref[...], (rows * SUB, LANES))
    rm[...] = jnp.full_like(rm, BIG)

    part = x_rows // 10

    def fill_x(c, carry):
        start = pl.multiple_of(c * part, 16)
        piece = xf[pl.ds(start, part + SUB), :]
        for m in range(SUB):
            x8[pl.ds(start, part), m * width : (m + 1) * width] = piece[m : m + part].astype(jnp.bfloat16)
        return carry

    lax.fori_loop(0, 10, fill_x, 0)

    def fill_y(c, carry):
        pieces = [yf[pl.ds(pl.multiple_of(h * tiles * SUB + c * SUB, SUB), 2 * SUB), :] for h in range(HIGH)]
        start = pl.multiple_of(c * LANES, LANES)
        for m in range(SUB):
            whole = jnp.concatenate([p[m : m + SUB] for p in pieces], 0)
            y8[pl.ds(start, LANES), m * width : (m + 1) * width] = whole.astype(jnp.bfloat16)
        return carry

    lax.fori_loop(0, 4 * steps, fill_y, 0)

    def multiply(k, s):
        first = (4 * k + 2 * s) * LANES
        out = gram[k % 2]
        out[LEAD * SUB :, 2 * s * LANES : 2 * (s + 1) * LANES] = lax.dot_general(
            x8[...], y8[first : first + 2 * LANES, :], (((1,), (1,)), ((), ())),
            preferred_element_type=jnp.float32,
        )

    def combine(k, s, mins):
        g = gram[k % 2]
        last = k >= 2
        if last:
            nbs = [jnp.broadcast_to(nb_ref[4 * k - 8 + j : 4 * k - 7 + j, :], (SUB, LANES)) for j in range(4)]
        waiting = {}

        def reg(ref, row, j=0):
            return ref[row * SUB : (row + 1) * SUB, j * LANES : (j + 1) * LANES]

        def settle(r):
            best = waiting.pop(r)
            at = slice((r + 16) * SUB, (r + 17) * SUB)
            rm[at, :] = jnp.minimum(rm[at, :], best)

        for i in range(s * half, (s + 1) * half):
            rho = i - LEAD
            d = slice((rho - 4 * k + shift0) * SUB, (rho - 4 * k + shift0 + 1) * SUB)
            gs = [reg(g, rho + LEAD + j, j) for j in range(4)]
            prev = gc[d, :]
            one = [prev + gs[0], gs[0] + gs[1], gs[1] + gs[2], gs[2] + gs[3]]
            two = [a1c[0][d, :] + one[0], a1c[1][d, :] + one[1], one[0] + one[2], one[1] + one[3]]
            if last:
                three = [a2c[j][d, :] + two[j] for j in range(4)]
                for j in range(4):
                    r = rho - 7 + j
                    if r < 0 or r >= rows:
                        continue
                    row_value = three[j] + nbs[j]
                    col_value = three[j] + nab[(r + 16) * SUB : (r + 17) * SUB, :]
                    mins[j] = col_value if mins[j] is None else jnp.minimum(mins[j], col_value)
                    waiting[r] = jnp.minimum(waiting[r], row_value) if r in waiting else row_value
                    if j == 0:
                        settle(r)
            if k < steps - 1:
                gc[d, :] = gs[3]
                a1c[0][d, :] = one[2]
                a1c[1][d, :] = one[3]
                for j in range(4):
                    a2c[j][d, :] = two[j]
        for r in sorted(waiting):
            settle(r)
        return mins

    multiply(0, 0)
    multiply(0, 1)
    for k in range(steps):
        if k == steps - 1:
            p = lax.broadcasted_iota(jnp.int32, (SPAN // 2, LANES), 0)
            lane = lax.broadcasted_iota(jnp.int32, (SPAN // 2, LANES), 1)
            for j in range(4):
                close = (lane >= LANES - SUB) & (p < SUB * j + lane - (LANES - SUB))
                at = (7 - j - 4 * k + shift0) * SUB
                a2c[j][at : at + SPAN // 2, :] += jnp.where(close, pen_ref[0, 0], 0.0)
        mins = [None] * 4
        for s in range(2):
            if k + 1 < steps:
                multiply(k + 1, s)
            mins = combine(k, s, mins)
        if k >= 2:
            for j in range(4):
                t = 4 * k - 8 + j
                co_ref[t : t + 1, :] = jnp.min(mins[j], axis=0, keepdims=True)
    scale = 1.0 / (SPAN * width)
    ro_ref[...] = jnp.minimum(
        (jnp.min(rm[16 * SUB : (16 + rows) * SUB, :], axis=1, keepdims=True) + na_ref[...]) * scale, CEIL
    )
    co_ref[...] = jnp.minimum((co_ref[...] + nb_ref[...]) * scale, CEIL)


def meet(x_ext, y_ext, na, nb, pen):
    row_count = na.shape[0]
    col_count = nb.shape[0]
    width = x_ext.shape[1]
    rows = row_count // SUB
    tiles = col_count // LANES
    steps = (tiles + 8) // 4
    x_rows = (rows + 12) * SUB
    x_rows = -(-x_rows // 160) * 160
    nb_t = nb.reshape(HIGH, tiles, SUB).transpose(1, 0, 2).reshape(tiles, LANES)
    deep = (rows + 12 + 4 * steps) * SUB
    f32 = jnp.float32
    vm = functools.partial(pltpu.VMEM)
    scratch = [
        vm((x_rows + 16, width), f32),
        vm((col_count + SPAN + 2 * SUB, width), f32),
        vm((x_rows, SUB * width), jnp.bfloat16),
        vm((4 * steps * LANES, SUB * width), jnp.bfloat16),
        vm((x_rows + LEAD * SUB, 4 * LANES), f32),
        vm((x_rows + LEAD * SUB, 4 * LANES), f32),
    ] + [vm((deep, LANES), f32)] * 7 + [vm(((rows + 32) * SUB, LANES), f32)] * 2
    ro, co = pl.pallas_call(
        functools.partial(meet_kernel, rows, tiles),
        out_shape=(jax.ShapeDtypeStruct((row_count, 1), f32), jax.ShapeDtypeStruct((tiles, LANES), f32)),
        in_specs=[pl.BlockSpec(memory_space=pltpu.VMEM)] * 4 + [pl.BlockSpec(memory_space=pltpu.SMEM)],
        out_specs=[pl.BlockSpec(memory_space=pltpu.VMEM)] * 2,
        scratch_shapes=scratch,
        compiler_params=pltpu.CompilerParams(vmem_limit_bytes=48 * 1024 * 1024),
        cost_estimate=pl.CostEstimate(flops=2 * row_count * col_count * SUB * width, bytes_accessed=2 << 20, transcendentals=0),
    )(x_ext, y_ext, na[:, None], nb_t, pen)
    return ro[:, 0], co.reshape(tiles, HIGH, SUB).transpose(1, 0, 2).reshape(col_count)


def meeting(own_ext, own_norm, me, partner, target, axis_name, seg_count):
    far_ext = lax.dynamic_slice_in_dim(
        lax.all_gather(own_ext, axis_name, axis=0, tiled=True), target * own_ext.shape[0], own_ext.shape[0], 0
    )
    far_norm = lax.dynamic_index_in_dim(lax.all_gather(own_norm, axis_name, axis=0), target, 0, keepdims=False)
    half = seg_count // 2
    lower = me < partner
    x_ext = jnp.where(lower, far_ext[: half + SPAN], own_ext[half:])
    y_ext = jnp.where(lower, own_ext, far_ext)
    na = jnp.where(lower, far_norm[:half], own_norm[half:])
    nb = jnp.where(lower, own_norm, far_norm)
    pen = jnp.where(lower & (partner == me + 1), BIG, 0.0).astype(jnp.float32).reshape(1, 1)
    across, down = meet(x_ext, y_ext, na, nb, pen)
    capped = jnp.full((half,), CEIL, jnp.float32)
    kept = jnp.where(lower, down, jnp.concatenate([capped, across]))
    outgoing = jnp.where(lower, jnp.concatenate([across, capped]), down)
    arrived = lax.dynamic_index_in_dim(
        lax.all_gather(outgoing, axis_name, axis=0), target, 0, keepdims=False
    )
    return jnp.minimum(kept, arrived)


def per_device(beats, track_marks, valid_beats, pairing):
    seg_count = beats.shape[0]
    col_count = lax.axis_size("col")
    total = valid_beats.shape[0]
    me = lax.axis_index("row") * col_count + lax.axis_index("col")
    marks = track_marks.astype(jnp.bfloat16)
    head_beats, head_marks = from_behind((beats[:SPAN], marks[:SPAN]), ("row", "col"), -1)
    own_ext = jnp.concatenate([beats, head_beats], 0)
    mark_ext = jnp.concatenate([marks, head_marks], 0).astype(jnp.float32)
    crossed = window_sum(mark_ext, seg_count) - mark_ext[:seg_count]
    offsets = jnp.arange(seg_count, dtype=jnp.int32)
    valid_here = valid_beats[me]
    within = offsets + (SPAN - 1) < valid_here
    crossing = (valid_here == seg_count) & (me < total - 1)
    live = (within | crossing) & (crossed < 0.5)
    own_sq = jnp.sum(jnp.square(own_ext.astype(jnp.float32)), axis=1)
    own_norm = jnp.where(live, window_sum(own_sq, seg_count), BIG)
    first = pairing[0, me]
    second = pairing[1, me]
    a = meeting(own_ext, own_norm, me, first, first // col_count, "row", seg_count)
    b = meeting(own_ext, own_norm, me, second, second % col_count, "col", seg_count)
    return jnp.minimum(a, b)


def solution(mesh):
    placed = (P(("row", "col"), None), P(("row", "col")), P(), P())
    return jax.shard_map(
        per_device, mesh=mesh, in_specs=placed, out_specs=P(("row", "col")), check_vma=False
    )
```

```python
import functools

import jax
import jax.numpy as jnp
from jax import lax
from jax.experimental import pallas as pl
from jax.experimental.pallas import tpu as pltpu
from jax.sharding import PartitionSpec as P

SPAN = 64
CEIL = 4.0
BIG = 1e9
LANES = 128
SUB = 8
HIGH = LANES // SUB
LEAD = 4


def from_behind(block, axis, distance):
    devices = range(lax.axis_size(axis))
    route = [(i - distance, i) for i in devices if i - distance in devices]
    return lax.ppermute(block, axis, route)


def window_sum(values, count):
    layered = values
    window = 1
    while window < SPAN:
        layered = layered[:-window] + layered[window:]
        window = window * 2
    return layered[:count]


def meet_kernel(
    rows, tiles, x_ref, y_ref, na_ref, nb_ref, pen_ref, ro_ref, co_ref,
    xf, yf, x8, y8, ga, gb, gc, a10, a11, a20, a21, a22, a23, nab, rm,
):
    width = x_ref.shape[1]
    x_rows = x8.shape[0]
    steps = (tiles + 8) // 4
    a1c = (a10, a11)
    a2c = (a20, a21, a22, a23)
    gram = (ga, gb)
    shift0 = 4 * steps
    chains = rows + 12
    half = chains // 2

    xf[...] = jnp.zeros_like(xf)
    xf[: x_ref.shape[0], :] = x_ref[...].astype(jnp.float32) * -2.0
    yf[:SUB, :] = jnp.zeros((SUB, width), jnp.float32)
    yf[SUB : SUB + y_ref.shape[0], :] = y_ref[...].astype(jnp.float32)
    for ref in (gc,) + a1c + a2c:
        ref[...] = jnp.zeros_like(ref)
    for ref in gram:
        ref[: LEAD * SUB, :] = jnp.zeros((LEAD * SUB, ref.shape[1]), jnp.float32)
    nab[...] = jnp.full_like(nab, BIG)
    nab[16 * SUB : (16 + rows) * SUB, :] = jnp.broadcast_to(na_ref[...], (rows * SUB, LANES))
    rm[...] = jnp.full_like(rm, BIG)

    part = x_rows // 10

    def fill_x(c, carry):
        start = pl.multiple_of(c * part, 16)
        piece = xf[pl.ds(start, part + SUB), :]
        for m in range(SUB):
            x8[pl.ds(start, part), m * width : (m + 1) * width] = piece[m : m + part].astype(jnp.bfloat16)
        return carry

    lax.fori_loop(0, 10, fill_x, 0)

    def fill_y(c, carry):
        pieces = [yf[pl.ds(pl.multiple_of(h * tiles * SUB + c * SUB, SUB), 2 * SUB), :] for h in range(HIGH)]
        start = pl.multiple_of(c * LANES, LANES)
        for m in range(SUB):
            whole = jnp.concatenate([p[m : m + SUB] for p in pieces], 0)
            y8[pl.ds(start, LANES), m * width : (m + 1) * width] = whole.astype(jnp.bfloat16)
        return carry

    lax.fori_loop(0, 4 * steps, fill_y, 0)

    def multiply(k, s):
        first = (4 * k + 2 * s) * LANES
        out = gram[k % 2]
        out[LEAD * SUB :, 2 * s * LANES : 2 * (s + 1) * LANES] = lax.dot_general(
            x8[...], y8[first : first + 2 * LANES, :], (((1,), (1,)), ((), ())),
            preferred_element_type=jnp.float32,
        )

    def combine(k, s, mins):
        g = gram[k % 2]
        last = k >= 2
        if last:
            nbs = [jnp.broadcast_to(nb_ref[4 * k - 8 + j : 4 * k - 7 + j, :], (SUB, LANES)) for j in range(4)]
        waiting = {}

        def reg(ref, row, j=0):
            return ref[row * SUB : (row + 1) * SUB, j * LANES : (j + 1) * LANES]

        def settle(r):
            best = waiting.pop(r)
            at = slice((r + 16) * SUB, (r + 17) * SUB)
            rm[at, :] = jnp.minimum(rm[at, :], best)

        for i in range(s * half, (s + 1) * half):
            rho = i - LEAD
            d = slice((rho - 4 * k + shift0) * SUB, (rho - 4 * k + shift0 + 1) * SUB)
            gs = [reg(g, rho + LEAD + j, j) for j in range(4)]
            prev = gc[d, :]
            one = [prev + gs[0], gs[0] + gs[1], gs[1] + gs[2], gs[2] + gs[3]]
            two = [a1c[0][d, :] + one[0], a1c[1][d, :] + one[1], one[0] + one[2], one[1] + one[3]]
            if last:
                three = [a2c[j][d, :] + two[j] for j in range(4)]
                for j in range(4):
                    r = rho - 7 + j
                    if r < 0 or r >= rows:
                        continue
                    row_value = three[j] + nbs[j]
                    col_value = three[j] + nab[(r + 16) * SUB : (r + 17) * SUB, :]
                    mins[j] = col_value if mins[j] is None else jnp.minimum(mins[j], col_value)
                    waiting[r] = jnp.minimum(waiting[r], row_value) if r in waiting else row_value
                    if j == 0:
                        settle(r)
            if k < steps - 1:
                gc[d, :] = gs[3]
                a1c[0][d, :] = one[2]
                a1c[1][d, :] = one[3]
                for j in range(4):
                    a2c[j][d, :] = two[j]
        for r in sorted(waiting):
            settle(r)
        return mins

    multiply(0, 0)
    multiply(0, 1)
    for k in range(steps):
        if k == steps - 1:
            p = lax.broadcasted_iota(jnp.int32, (SPAN // 2, LANES), 0)
            lane = lax.broadcasted_iota(jnp.int32, (SPAN // 2, LANES), 1)
            for j in range(4):
                close = (lane >= LANES - SUB) & (p < SUB * j + lane - (LANES - SUB))
                at = (7 - j - 4 * k + shift0) * SUB
                a2c[j][at : at + SPAN // 2, :] += jnp.where(close, pen_ref[0, 0], 0.0)
        mins = [None] * 4
        for s in range(2):
            if k + 1 < steps:
                multiply(k + 1, s)
            mins = combine(k, s, mins)
        if k >= 2:
            for j in range(4):
                t = 4 * k - 8 + j
                co_ref[t : t + 1, :] = jnp.min(mins[j], axis=0, keepdims=True)
    scale = 1.0 / (SPAN * width)
    ro_ref[...] = jnp.minimum(
        (jnp.min(rm[16 * SUB : (16 + rows) * SUB, :], axis=1, keepdims=True) + na_ref[...]) * scale, CEIL
    )
    co_ref[...] = jnp.minimum((co_ref[...] + nb_ref[...]) * scale, CEIL)


def meet(x_ext, y_ext, na, nb, pen):
    row_count = na.shape[0]
    col_count = nb.shape[0]
    width = x_ext.shape[1]
    rows = row_count // SUB
    tiles = col_count // LANES
    steps = (tiles + 8) // 4
    x_rows = (rows + 12) * SUB
    x_rows = -(-x_rows // 160) * 160
    nb_t = nb.reshape(HIGH, tiles, SUB).transpose(1, 0, 2).reshape(tiles, LANES)
    deep = (rows + 12 + 4 * steps) * SUB
    f32 = jnp.float32
    vm = functools.partial(pltpu.VMEM)
    scratch = [
        vm((x_rows + 16, width), f32),
        vm((col_count + SPAN + 2 * SUB, width), f32),
        vm((x_rows, SUB * width), jnp.bfloat16),
        vm((4 * steps * LANES, SUB * width), jnp.bfloat16),
        vm((x_rows + LEAD * SUB, 4 * LANES), f32),
        vm((x_rows + LEAD * SUB, 4 * LANES), f32),
    ] + [vm((deep, LANES), f32)] * 7 + [vm(((rows + 32) * SUB, LANES), f32)] * 2
    ro, co = pl.pallas_call(
        functools.partial(meet_kernel, rows, tiles),
        out_shape=(jax.ShapeDtypeStruct((row_count, 1), f32), jax.ShapeDtypeStruct((tiles, LANES), f32)),
        in_specs=[pl.BlockSpec(memory_space=pltpu.VMEM)] * 4 + [pl.BlockSpec(memory_space=pltpu.SMEM)],
        out_specs=[pl.BlockSpec(memory_space=pltpu.VMEM)] * 2,
        scratch_shapes=scratch,
        compiler_params=pltpu.CompilerParams(vmem_limit_bytes=48 * 1024 * 1024),
        cost_estimate=pl.CostEstimate(flops=2 * row_count * col_count * SUB * width, bytes_accessed=2 << 20, transcendentals=0),
    )(x_ext, y_ext, na[:, None], nb_t, pen)
    return ro[:, 0], co.reshape(tiles, HIGH, SUB).transpose(1, 0, 2).reshape(col_count)


def gather_kernel(ext, norm, row_ext, row_norm, col_ext, col_norm, send, col_send, row_recv, col_recv):
    row_size, col_size = lax.axis_size("row"), lax.axis_size("col")
    row, col = lax.axis_index("row"), lax.axis_index("col")
    chips = col_size // 2
    chip, core = col // 2, col % 2
    sibling = 2 * chip + 1 - core
    has_right, has_left = chip + 1 < chips, chip > 0
    barrier = pltpu.get_barrier_semaphore()

    def greet(target):
        pl.semaphore_signal(barrier, inc=1, device_id=target, device_id_type=pl.DeviceIdType.MESH)

    for d in range(1, row_size):
        greet((lax.rem(row + d, row_size), col))
    for d in range(1, col_size):
        greet((row, lax.rem(col + d, col_size)))
    pl.semaphore_wait(barrier, row_size + col_size - 2)

    def moves(origin, way, own):
        slot = 2 * origin + core
        target = (row, sibling if way == 2 else col + 2 - 4 * way)
        return [
            pltpu.make_async_remote_copy(
                src_ref=whole if own else parts.at[slot],
                dst_ref=parts.at[slot],
                send_sem=col_send.at[n, way, origin],
                recv_sem=col_recv.at[n, slot],
                device_id=target,
                device_id_type=pl.DeviceIdType.MESH,
            )
            for n, (whole, parts) in enumerate(((ext, col_ext), (norm, col_norm)))
        ]

    def arrivals(slot):
        for n, (whole, parts) in enumerate(((ext, col_ext), (norm, col_norm))):
            pltpu.make_async_remote_copy(
                src_ref=whole,
                dst_ref=parts.at[slot],
                send_sem=col_send.at[n, 0, 0],
                recv_sem=col_recv.at[n, slot],
                device_id=(row, sibling),
                device_id_type=pl.DeviceIdType.MESH,
            ).wait_recv()

    def start(origin, way, own=False):
        for move in moves(origin, way, own):
            move.start()

    def sent(origin, way, own=False):
        for move in moves(origin, way, own):
            move.wait_send()

    def row_moves(d):
        target = lax.rem(row + d, row_size)
        return [
            pltpu.make_async_remote_copy(
                src_ref=whole,
                dst_ref=parts.at[row],
                send_sem=send.at[n, d],
                recv_sem=row_recv.at[n, d],
                device_id=(target, col),
                device_id_type=pl.DeviceIdType.MESH,
            )
            for n, (whole, parts) in enumerate(((ext, row_ext), (norm, row_norm)))
        ]

    pl.when(has_right)(lambda: start(chip, 0, True))
    pl.when(has_left)(lambda: start(chip, 1, True))
    for d in range(1, row_size):
        for move in row_moves(d):
            move.start()
    start(chip, 2, True)
    for s in range(1, chips):

        @pl.when(chip - s >= 0)
        def _():
            arrivals(2 * (chip - s) + core)
            pl.when(has_right)(lambda: start(chip - s, 0))
            start(chip - s, 2)

        @pl.when(chip + s < chips)
        def _():
            arrivals(2 * (chip + s) + core)
            pl.when(has_left)(lambda: start(chip + s, 1))
            start(chip + s, 2)

    for origin in range(chips):
        arrivals(2 * origin + 1 - core)
    for d in range(1, row_size):
        source = lax.rem(row + row_size - d, row_size)
        for n, (whole, parts) in enumerate(((ext, row_ext), (norm, row_norm))):
            pltpu.make_async_remote_copy(
                src_ref=whole,
                dst_ref=parts.at[source],
                send_sem=send.at[n, d],
                recv_sem=row_recv.at[n, d],
                device_id=(source, col),
                device_id_type=pl.DeviceIdType.MESH,
            ).wait_recv()
        for move in row_moves(d):
            move.wait_send()
    pl.when(has_right)(lambda: sent(chip, 0, True))
    pl.when(has_left)(lambda: sent(chip, 1, True))
    sent(chip, 2, True)
    for s in range(1, chips):

        @pl.when(chip - s >= 0)
        def _():
            pl.when(has_right)(lambda: sent(chip - s, 0))
            sent(chip - s, 2)

        @pl.when(chip + s < chips)
        def _():
            pl.when(has_left)(lambda: sent(chip + s, 1))
            sent(chip + s, 2)


def gather(ext, norm):
    row_size, col_size = lax.axis_size("row"), lax.axis_size("col")
    shapes = [
        jax.ShapeDtypeStruct((size,) + v.shape, v.dtype) for size in (row_size, col_size) for v in (ext, norm)
    ]
    return pl.pallas_call(
        gather_kernel,
        out_shape=tuple(shapes),
        in_specs=[pl.BlockSpec(memory_space=pl.ANY)] * 2,
        out_specs=[pl.BlockSpec(memory_space=pl.ANY)] * 4,
        scratch_shapes=[
            pltpu.SemaphoreType.DMA((2, row_size)),
            pltpu.SemaphoreType.DMA((2, 3, col_size // 2)),
            pltpu.SemaphoreType.DMA((2, row_size)),
            pltpu.SemaphoreType.DMA((2, col_size)),
        ],
        compiler_params=pltpu.CompilerParams(collective_id=0, has_side_effects=True),
    )(ext, norm)


def exchange_kernel(first, second, from_row, from_col, row_send, col_send, row_recv, col_recv):
    row_size, col_size = lax.axis_size("row"), lax.axis_size("col")
    row, col = lax.axis_index("row"), lax.axis_index("col")
    barrier = pltpu.get_barrier_semaphore()
    groups = (
        (row, row_size, first, from_row, row_send, row_recv, lambda i: (i, col)),
        (col, col_size, second, from_col, col_send, col_recv, lambda i: (row, i)),
    )
    for me, size, _, _, _, _, place in groups:
        for d in range(1, size):
            pl.semaphore_signal(
                barrier, inc=1, device_id=place(lax.rem(me + d, size)), device_id_type=pl.DeviceIdType.MESH
            )
    pl.semaphore_wait(barrier, row_size + col_size - 2)

    def move(group, d, slot, target):
        _, _, source, landing, send, recv, place = group
        return pltpu.make_async_remote_copy(
            src_ref=source,
            dst_ref=landing.at[slot],
            send_sem=send.at[d],
            recv_sem=recv.at[d],
            device_id=place(target),
            device_id_type=pl.DeviceIdType.MESH,
        )

    for group in groups:
        me, size = group[:2]
        for d in range(1, size):
            move(group, d, me, lax.rem(me + d, size)).start()
    for group in groups:
        me, size = group[:2]
        for d in range(1, size):
            source = lax.rem(me + size - d, size)
            move(group, d, source, source).wait_recv()
            move(group, d, me, lax.rem(me + d, size)).wait_send()


def exchange(first, second):
    row_size, col_size = lax.axis_size("row"), lax.axis_size("col")
    sems = [pltpu.SemaphoreType.DMA((n,)) for n in (row_size, col_size)]
    return pl.pallas_call(
        exchange_kernel,
        out_shape=tuple(jax.ShapeDtypeStruct((n,) + first.shape, first.dtype) for n in (row_size, col_size)),
        in_specs=[pl.BlockSpec(memory_space=pltpu.VMEM)] * 2,
        out_specs=[pl.BlockSpec(memory_space=pltpu.VMEM)] * 2,
        scratch_shapes=sems + sems,
        compiler_params=pltpu.CompilerParams(collective_id=1, has_side_effects=True),
    )(first, second)


def meeting(own_ext, own_norm, me, partner, target, far_exts, far_norms, seg_count):
    far_ext = lax.dynamic_index_in_dim(far_exts, target, 0, keepdims=False)
    far_norm = lax.dynamic_index_in_dim(far_norms, target, 0, keepdims=False).reshape(seg_count)
    half = seg_count // 2
    lower = me < partner
    x_ext = jnp.where(lower, far_ext[: half + SPAN], own_ext[half:])
    y_ext = jnp.where(lower, own_ext, far_ext)
    na = jnp.where(lower, far_norm[:half], own_norm[half:])
    nb = jnp.where(lower, own_norm, far_norm)
    pen = jnp.where(lower & (partner == me + 1), BIG, 0.0).astype(jnp.float32).reshape(1, 1)
    across, down = meet(x_ext, y_ext, na, nb, pen)
    capped = jnp.full((half,), CEIL, jnp.float32)
    kept = jnp.where(lower, down, jnp.concatenate([capped, across]))
    outgoing = jnp.where(lower, jnp.concatenate([across, capped]), down)
    return kept, outgoing.reshape(seg_count // LANES, LANES)


def per_device(beats, track_marks, valid_beats, pairing):
    seg_count = beats.shape[0]
    col_count = lax.axis_size("col")
    total = valid_beats.shape[0]
    me = lax.axis_index("row") * col_count + lax.axis_index("col")
    marks = track_marks.astype(jnp.bfloat16)
    head_beats, head_marks = from_behind((beats[:SPAN], marks[:SPAN]), ("row", "col"), -1)
    own_ext = jnp.concatenate([beats, head_beats], 0)
    mark_ext = jnp.concatenate([marks, head_marks], 0).astype(jnp.float32)
    crossed = window_sum(mark_ext, seg_count) - mark_ext[:seg_count]
    offsets = jnp.arange(seg_count, dtype=jnp.int32)
    valid_here = valid_beats[me]
    within = offsets + (SPAN - 1) < valid_here
    crossing = (valid_here == seg_count) & (me < total - 1)
    live = (within | crossing) & (crossed < 0.5)
    own_sq = jnp.sum(jnp.square(own_ext.astype(jnp.float32)), axis=1)
    own_norm = jnp.where(live, window_sum(own_sq, seg_count), BIG)
    first = pairing[0, me]
    second = pairing[1, me]
    to_row, to_col = first // col_count, second % col_count
    row_ext, row_norm, col_ext, col_norm = gather(own_ext, own_norm.reshape(seg_count // LANES, LANES))
    kept_a, out_a = meeting(own_ext, own_norm, me, first, to_row, row_ext, row_norm, seg_count)
    kept_b, out_b = meeting(own_ext, own_norm, me, second, to_col, col_ext, col_norm, seg_count)
    from_row, from_col = exchange(out_a, out_b)
    near = jnp.minimum(
        lax.dynamic_index_in_dim(from_row, to_row, 0, keepdims=False),
        lax.dynamic_index_in_dim(from_col, to_col, 0, keepdims=False),
    )
    return jnp.minimum(jnp.minimum(kept_a, kept_b), near.reshape(seg_count))


def solution(mesh):
    placed = (P(("row", "col"), None), P(("row", "col")), P(), P())
    return jax.shard_map(
        per_device, mesh=mesh, in_specs=placed, out_specs=P(("row", "col")), check_vma=False
    )
```

```python
import functools

import jax
import jax.numpy as jnp
from jax import lax
from jax.experimental import pallas as pl
from jax.experimental.pallas import tpu as pltpu
from jax.sharding import PartitionSpec as P

SPAN = 64
CEIL = 4.0
BIG = 1e9
LANES = 128
SUB = 8
HIGH = LANES // SUB
LEAD = 4


def from_behind(block, axis, distance):
    devices = range(lax.axis_size(axis))
    route = [(i - distance, i) for i in devices if i - distance in devices]
    return lax.ppermute(block, axis, route)


def window_sum(values, count):
    layered = values
    window = 1
    while window < SPAN:
        layered = layered[:, :-window] + layered[:, window:]
        window = window * 2
    return layered[:, :count]


def meet_kernel(
    rows, tiles, x_ref, y_ref, na_ref, nb_ref, pen_ref, ro_ref, co_ref,
    xf, yf, x8, y8, ga, gb, gc, a10, a11, a20, a21, a22, a23, nab, rm,
):
    width = x_ref.shape[1]
    x_rows = x8.shape[0]
    steps = (tiles + 8) // 4
    a1c = (a10, a11)
    a2c = (a20, a21, a22, a23)
    gram = (ga, gb)
    shift0 = 4 * steps
    chains = rows + 12
    half = chains // 2

    xf[...] = jnp.zeros_like(xf)
    xf[: x_ref.shape[0], :] = x_ref[...].astype(jnp.float32) * -2.0
    yf[:SUB, :] = jnp.zeros((SUB, width), jnp.float32)
    yf[SUB : SUB + y_ref.shape[0], :] = y_ref[...].astype(jnp.float32)
    for ref in (gc,) + a1c + a2c:
        ref[...] = jnp.zeros_like(ref)
    for ref in gram:
        ref[: LEAD * SUB, :] = jnp.zeros((LEAD * SUB, ref.shape[1]), jnp.float32)
    nab[...] = jnp.full_like(nab, BIG)
    nab[16 * SUB : (16 + rows) * SUB, :] = jnp.broadcast_to(na_ref[...], (rows * SUB, LANES))
    rm[...] = jnp.full_like(rm, BIG)

    part = x_rows // 10

    def fill_x(c, carry):
        start = pl.multiple_of(c * part, 16)
        piece = xf[pl.ds(start, part + SUB), :]
        for m in range(SUB):
            x8[pl.ds(start, part), m * width : (m + 1) * width] = piece[m : m + part].astype(jnp.bfloat16)
        return carry

    lax.fori_loop(0, 10, fill_x, 0)

    def fill_y(c, carry):
        pieces = [yf[pl.ds(pl.multiple_of(h * tiles * SUB + c * SUB, SUB), 2 * SUB), :] for h in range(HIGH)]
        start = pl.multiple_of(c * LANES, LANES)
        for m in range(SUB):
            whole = jnp.concatenate([p[m : m + SUB] for p in pieces], 0)
            y8[pl.ds(start, LANES), m * width : (m + 1) * width] = whole.astype(jnp.bfloat16)
        return carry

    lax.fori_loop(0, 4 * steps, fill_y, 0)

    def multiply(k, s):
        first = (4 * k + 2 * s) * LANES
        out = gram[k % 2]
        out[LEAD * SUB :, 2 * s * LANES : 2 * (s + 1) * LANES] = lax.dot_general(
            x8[...], y8[first : first + 2 * LANES, :], (((1,), (1,)), ((), ())),
            preferred_element_type=jnp.float32,
        )

    def combine(k, s, mins):
        g = gram[k % 2]
        last = k >= 2
        if last:
            nbs = [jnp.broadcast_to(nb_ref[4 * k - 8 + j : 4 * k - 7 + j, :], (SUB, LANES)) for j in range(4)]
        waiting = {}

        def reg(ref, row, j=0):
            return ref[row * SUB : (row + 1) * SUB, j * LANES : (j + 1) * LANES]

        def settle(r):
            best = waiting.pop(r)
            at = slice((r + 16) * SUB, (r + 17) * SUB)
            rm[at, :] = jnp.minimum(rm[at, :], best)

        for i in range(s * half, (s + 1) * half):
            rho = i - LEAD
            d = slice((rho - 4 * k + shift0) * SUB, (rho - 4 * k + shift0 + 1) * SUB)
            gs = [reg(g, rho + LEAD + j, j) for j in range(4)]
            prev = gc[d, :]
            one = [prev + gs[0], gs[0] + gs[1], gs[1] + gs[2], gs[2] + gs[3]]
            two = [a1c[0][d, :] + one[0], a1c[1][d, :] + one[1], one[0] + one[2], one[1] + one[3]]
            if last:
                three = [a2c[j][d, :] + two[j] for j in range(4)]
                for j in range(4):
                    r = rho - 7 + j
                    if r < 0 or r >= rows:
                        continue
                    row_value = three[j] + nbs[j]
                    col_value = three[j] + nab[(r + 16) * SUB : (r + 17) * SUB, :]
                    mins[j] = col_value if mins[j] is None else jnp.minimum(mins[j], col_value)
                    waiting[r] = jnp.minimum(waiting[r], row_value) if r in waiting else row_value
                    if j == 0:
                        settle(r)
            if k < steps - 1:
                gc[d, :] = gs[3]
                a1c[0][d, :] = one[2]
                a1c[1][d, :] = one[3]
                for j in range(4):
                    a2c[j][d, :] = two[j]
        for r in sorted(waiting):
            settle(r)
        return mins

    multiply(0, 0)
    multiply(0, 1)
    for k in range(steps):
        if k == steps - 1:
            p = lax.broadcasted_iota(jnp.int32, (SPAN // 2, LANES), 0)
            lane = lax.broadcasted_iota(jnp.int32, (SPAN // 2, LANES), 1)
            for j in range(4):
                close = (lane >= LANES - SUB) & (p < SUB * j + lane - (LANES - SUB))
                at = (7 - j - 4 * k + shift0) * SUB
                a2c[j][at : at + SPAN // 2, :] += jnp.where(close, pen_ref[0, 0], 0.0)
        mins = [None] * 4
        for s in range(2):
            if k + 1 < steps:
                multiply(k + 1, s)
            mins = combine(k, s, mins)
        if k >= 2:
            for j in range(4):
                t = 4 * k - 8 + j
                co_ref[t : t + 1, :] = jnp.min(mins[j], axis=0, keepdims=True)
    scale = 1.0 / (SPAN * width)
    ro_ref[...] = jnp.minimum(
        (jnp.min(rm[16 * SUB : (16 + rows) * SUB, :], axis=1, keepdims=True) + na_ref[...]) * scale, CEIL
    )
    co_ref[...] = jnp.minimum((co_ref[...] + nb_ref[...]) * scale, CEIL)


def meet(x_ext, y_ext, na, nb, pen):
    row_count = na.shape[0]
    col_count = nb.shape[0]
    width = x_ext.shape[1]
    rows = row_count // SUB
    tiles = col_count // LANES
    steps = (tiles + 8) // 4
    x_rows = (rows + 12) * SUB
    x_rows = -(-x_rows // 160) * 160
    nb_t = nb.reshape(HIGH, tiles, SUB).transpose(1, 0, 2).reshape(tiles, LANES)
    deep = (rows + 12 + 4 * steps) * SUB
    f32 = jnp.float32
    vm = functools.partial(pltpu.VMEM)
    scratch = [
        vm((x_rows + 16, width), f32),
        vm((col_count + SPAN + 2 * SUB, width), f32),
        vm((x_rows, SUB * width), jnp.bfloat16),
        vm((4 * steps * LANES, SUB * width), jnp.bfloat16),
        vm((x_rows + LEAD * SUB, 4 * LANES), f32),
        vm((x_rows + LEAD * SUB, 4 * LANES), f32),
    ] + [vm((deep, LANES), f32)] * 7 + [vm(((rows + 32) * SUB, LANES), f32)] * 2
    ro, co = pl.pallas_call(
        functools.partial(meet_kernel, rows, tiles),
        out_shape=(jax.ShapeDtypeStruct((row_count, 1), f32), jax.ShapeDtypeStruct((tiles, LANES), f32)),
        in_specs=[pl.BlockSpec(memory_space=pltpu.VMEM)] * 4 + [pl.BlockSpec(memory_space=pltpu.SMEM)],
        out_specs=[pl.BlockSpec(memory_space=pltpu.VMEM)] * 2,
        scratch_shapes=scratch,
        compiler_params=pltpu.CompilerParams(vmem_limit_bytes=48 * 1024 * 1024),
        cost_estimate=pl.CostEstimate(flops=2 * row_count * col_count * SUB * width, bytes_accessed=2 << 20, transcendentals=0),
    )(x_ext, y_ext, na[:, None], nb_t, pen)
    return ro[:, 0], co.reshape(tiles, HIGH, SUB).transpose(1, 0, 2).reshape(col_count)


def gather_kernel(ext, norm, row_ext, row_norm, col_ext, col_norm, send, col_send, row_recv, col_recv):
    row_size, col_size = lax.axis_size("row"), lax.axis_size("col")
    row, col = lax.axis_index("row"), lax.axis_index("col")
    chips = col_size // 2
    chip, core = col // 2, col % 2
    sibling = 2 * chip + 1 - core
    has_right, has_left = chip + 1 < chips, chip > 0
    barrier = pltpu.get_barrier_semaphore()

    def greet(target):
        pl.semaphore_signal(barrier, inc=1, device_id=target, device_id_type=pl.DeviceIdType.MESH)

    for d in range(1, row_size):
        greet((lax.rem(row + d, row_size), col))
    for d in range(1, col_size):
        greet((row, lax.rem(col + d, col_size)))
    pl.semaphore_wait(barrier, row_size + col_size - 2)

    def moves(origin, way, own):
        slot = 2 * origin + core
        target = (row, sibling if way == 2 else col + 2 - 4 * way)
        return [
            pltpu.make_async_remote_copy(
                src_ref=whole if own else parts.at[slot],
                dst_ref=parts.at[slot],
                send_sem=col_send.at[n, way, origin],
                recv_sem=col_recv.at[n, slot],
                device_id=target,
                device_id_type=pl.DeviceIdType.MESH,
            )
            for n, (whole, parts) in enumerate(((ext, col_ext), (norm, col_norm)))
        ]

    def arrivals(slot):
        for n, (whole, parts) in enumerate(((ext, col_ext), (norm, col_norm))):
            pltpu.make_async_remote_copy(
                src_ref=whole,
                dst_ref=parts.at[slot],
                send_sem=col_send.at[n, 0, 0],
                recv_sem=col_recv.at[n, slot],
                device_id=(row, sibling),
                device_id_type=pl.DeviceIdType.MESH,
            ).wait_recv()

    def start(origin, way, own=False):
        for move in moves(origin, way, own):
            move.start()

    def sent(origin, way, own=False):
        for move in moves(origin, way, own):
            move.wait_send()

    def row_moves(d):
        target = lax.rem(row + d, row_size)
        return [
            pltpu.make_async_remote_copy(
                src_ref=whole,
                dst_ref=parts.at[row],
                send_sem=send.at[n, d],
                recv_sem=row_recv.at[n, d],
                device_id=(target, col),
                device_id_type=pl.DeviceIdType.MESH,
            )
            for n, (whole, parts) in enumerate(((ext, row_ext), (norm, row_norm)))
        ]

    pl.when(has_right)(lambda: start(chip, 0, True))
    pl.when(has_left)(lambda: start(chip, 1, True))
    for d in range(1, row_size):
        for move in row_moves(d):
            move.start()
    start(chip, 2, True)
    for s in range(1, chips):

        @pl.when(chip - s >= 0)
        def _():
            arrivals(2 * (chip - s) + core)
            pl.when(has_right)(lambda: start(chip - s, 0))
            start(chip - s, 2)

        @pl.when(chip + s < chips)
        def _():
            arrivals(2 * (chip + s) + core)
            pl.when(has_left)(lambda: start(chip + s, 1))
            start(chip + s, 2)

    for origin in range(chips):
        arrivals(2 * origin + 1 - core)
    for d in range(1, row_size):
        source = lax.rem(row + row_size - d, row_size)
        for n, (whole, parts) in enumerate(((ext, row_ext), (norm, row_norm))):
            pltpu.make_async_remote_copy(
                src_ref=whole,
                dst_ref=parts.at[source],
                send_sem=send.at[n, d],
                recv_sem=row_recv.at[n, d],
                device_id=(source, col),
                device_id_type=pl.DeviceIdType.MESH,
            ).wait_recv()
        for move in row_moves(d):
            move.wait_send()
    pl.when(has_right)(lambda: sent(chip, 0, True))
    pl.when(has_left)(lambda: sent(chip, 1, True))
    sent(chip, 2, True)
    for s in range(1, chips):

        @pl.when(chip - s >= 0)
        def _():
            pl.when(has_right)(lambda: sent(chip - s, 0))
            sent(chip - s, 2)

        @pl.when(chip + s < chips)
        def _():
            pl.when(has_left)(lambda: sent(chip + s, 1))
            sent(chip + s, 2)


def gather(ext, norm):
    row_size, col_size = lax.axis_size("row"), lax.axis_size("col")
    shapes = [
        jax.ShapeDtypeStruct((size,) + v.shape, v.dtype) for size in (row_size, col_size) for v in (ext, norm)
    ]
    return pl.pallas_call(
        gather_kernel,
        out_shape=tuple(shapes),
        in_specs=[pl.BlockSpec(memory_space=pl.ANY)] * 2,
        out_specs=[pl.BlockSpec(memory_space=pl.ANY)] * 4,
        scratch_shapes=[
            pltpu.SemaphoreType.DMA((2, row_size)),
            pltpu.SemaphoreType.DMA((2, 3, col_size // 2)),
            pltpu.SemaphoreType.DMA((2, row_size)),
            pltpu.SemaphoreType.DMA((2, col_size)),
        ],
        compiler_params=pltpu.CompilerParams(collective_id=0, has_side_effects=True),
    )(ext, norm)


def exchange_kernel(first, second, from_row, from_col, row_send, col_send, row_recv, col_recv):
    row_size, col_size = lax.axis_size("row"), lax.axis_size("col")
    row, col = lax.axis_index("row"), lax.axis_index("col")
    barrier = pltpu.get_barrier_semaphore()
    groups = (
        (row, row_size, first, from_row, row_send, row_recv, lambda i: (i, col)),
        (col, col_size, second, from_col, col_send, col_recv, lambda i: (row, i)),
    )
    for me, size, _, _, _, _, place in groups:
        for d in range(1, size):
            pl.semaphore_signal(
                barrier, inc=1, device_id=place(lax.rem(me + d, size)), device_id_type=pl.DeviceIdType.MESH
            )
    pl.semaphore_wait(barrier, row_size + col_size - 2)

    def move(group, d, slot, target):
        _, _, source, landing, send, recv, place = group
        return pltpu.make_async_remote_copy(
            src_ref=source,
            dst_ref=landing.at[slot],
            send_sem=send.at[d],
            recv_sem=recv.at[d],
            device_id=place(target),
            device_id_type=pl.DeviceIdType.MESH,
        )

    for group in groups:
        me, size = group[:2]
        for d in range(1, size):
            move(group, d, me, lax.rem(me + d, size)).start()
    for group in groups:
        me, size = group[:2]
        for d in range(1, size):
            source = lax.rem(me + size - d, size)
            move(group, d, source, source).wait_recv()
            move(group, d, me, lax.rem(me + d, size)).wait_send()


def exchange(first, second):
    row_size, col_size = lax.axis_size("row"), lax.axis_size("col")
    sems = [pltpu.SemaphoreType.DMA((n,)) for n in (row_size, col_size)]
    return pl.pallas_call(
        exchange_kernel,
        out_shape=tuple(jax.ShapeDtypeStruct((n,) + first.shape, first.dtype) for n in (row_size, col_size)),
        in_specs=[pl.BlockSpec(memory_space=pltpu.VMEM)] * 2,
        out_specs=[pl.BlockSpec(memory_space=pltpu.VMEM)] * 2,
        scratch_shapes=sems + sems,
        compiler_params=pltpu.CompilerParams(collective_id=1, has_side_effects=True),
    )(first, second)


def meeting(own_ext, own_norm, me, partner, target, far_exts, far_norms, seg_count):
    far_ext = lax.dynamic_index_in_dim(far_exts, target, 0, keepdims=False)
    far_norm = lax.dynamic_index_in_dim(far_norms, target, 0, keepdims=False).reshape(seg_count)
    half = seg_count // 2
    lower = me < partner
    x_ext = jnp.where(lower, far_ext[: half + SPAN], own_ext[half:])
    y_ext = jnp.where(lower, own_ext, far_ext)
    na = jnp.where(lower, far_norm[:half], own_norm[half:])
    nb = jnp.where(lower, own_norm, far_norm)
    pen = jnp.where(lower & (partner == me + 1), BIG, 0.0).astype(jnp.float32).reshape(1, 1)
    across, down = meet(x_ext, y_ext, na, nb, pen)
    capped = jnp.full((half,), CEIL, jnp.float32)
    kept = jnp.where(lower, down, jnp.concatenate([capped, across]))
    outgoing = jnp.where(lower, jnp.concatenate([across, capped]), down)
    return kept, outgoing.reshape(seg_count // LANES, LANES)


def per_device(beats, track_marks, valid_beats, pairing):
    seg_count = beats.shape[0]
    col_count = lax.axis_size("col")
    total = valid_beats.shape[0]
    me = lax.axis_index("row") * col_count + lax.axis_index("col")
    marks = track_marks.astype(jnp.bfloat16)
    head_beats, head_marks = from_behind((beats[:SPAN], marks[:SPAN]), ("row", "col"), -1)
    own_ext = jnp.concatenate([beats, head_beats], 0)
    mark_ext = jnp.concatenate([marks, head_marks], 0).astype(jnp.float32)
    own_sq = jnp.sum(jnp.square(own_ext.astype(jnp.float32)), axis=1)
    marked, norms = window_sum(jnp.stack([mark_ext, own_sq]), seg_count)
    crossed = marked - mark_ext[:seg_count]
    offsets = jnp.arange(seg_count, dtype=jnp.int32)
    valid_here = valid_beats[me]
    within = offsets + (SPAN - 1) < valid_here
    crossing = (valid_here == seg_count) & (me < total - 1)
    live = (within | crossing) & (crossed < 0.5)
    own_norm = jnp.where(live, norms, BIG)
    first = pairing[0, me]
    second = pairing[1, me]
    to_row, to_col = first // col_count, second % col_count
    row_ext, row_norm, col_ext, col_norm = gather(own_ext, own_norm.reshape(seg_count // LANES, LANES))
    kept_a, out_a = meeting(own_ext, own_norm, me, first, to_row, row_ext, row_norm, seg_count)
    kept_b, out_b = meeting(own_ext, own_norm, me, second, to_col, col_ext, col_norm, seg_count)
    from_row, from_col = exchange(out_a, out_b)
    near = jnp.minimum(
        lax.dynamic_index_in_dim(from_row, to_row, 0, keepdims=False),
        lax.dynamic_index_in_dim(from_col, to_col, 0, keepdims=False),
    )
    return jnp.minimum(jnp.minimum(kept_a, kept_b), near.reshape(seg_count))


def solution(mesh):
    placed = (P(("row", "col"), None), P(("row", "col")), P(), P())
    return jax.shard_map(
        per_device, mesh=mesh, in_specs=placed, out_specs=P(("row", "col")), check_vma=False
    )
```
